32 devices in a mesh: row: 4 (over y, x), col: 8 (over z, core).
Axes of the slice: x: 2, y: 2, z: 4, core: 2. Of those that a mesh axis runs over, the one named last changes fastest.
Arguments:
- features: bfloat16 [8, 2048, 128], P('col'), may hold values from -6 to 6
- dst_features: bfloat16 [4096, 128], P(('row', 'col')), may hold values from -6 to 6
- w_self: bfloat16 [128, 256], replicated, may hold values from -0.5 to 0.5
- w_neigh: bfloat16 [128, 256], replicated, may hold values from -0.5 to 0.5
- cotangent: bfloat16 [4096, 256], P(('row', 'col')), may hold values from -6 to 6
- block_values: bfloat16 [4, 8, 32, 128, 128], P('row', 'col'), may hold values from -0.15625 to 0.15625
- block_rows: int32 [4, 8, 32], P('row', 'col'), may hold values from 0 to 7, as said below
- block_cols: int32 [4, 8, 32], P('row', 'col'), may hold values from 0 to 15
- block_counts: int32 [4, 8], P('row', 'col'), may hold values from 4 to 32, as said below
Outputs:
- output: bfloat16 [4096, 256], P(('row', 'col'))
- grad_w_self: float32 [128, 256], replicated
- grad_w_neigh: float32 [128, 256], replicated
- grad_features: float32 [8, 2048, 128], P('col', 'row')
The draws below stay inside these ranges and needn't reach their ends.
Inputs may be any that keep to these rules, and one draw needn't show every extreme that they name: On one device the slots name distinct pairs of block_rows and block_cols, also in unused slots. `block_counts`: some device uses all 32 slots in every draw.
All inputs are finite; a program needn't handle non-finite values.
Results may differ from the reference program's by a relative error of at most 0.0052.
Values may be sent and summed in bfloat16 or wider, within the bound.
No kernel may reach another device: no remote copies, remote signals or barrier semaphores. Data moves between devices by JAX's collectives and lax.ppermute only.
A program may use at most 64 MiB of HBM per device.

```python
import math
import jax
import jax.numpy as jnp
from jax import lax

F = 128
H = 256
BLOCK = 128
DST_DEV = 128
CB = 16
SLOTS = 32
RB = 8
DST = 4096
N_ROW = 4
N_COL = 8


def slot_table(key):
    base_key = jax.random.fold_in(key, 7)
    device_keys = jax.random.split(base_key, N_ROW * N_COL)

    def one_device(device_key):
        return jax.random.permutation(device_key, RB * CB)[:SLOTS]
    chosen = jax.vmap(one_device)(device_keys)
    return chosen.reshape(N_ROW, N_COL, SLOTS).astype(jnp.int32)


def draw_block_rows(key, part):
    return slot_table(key) // CB


def draw_block_cols(key, part):
    return slot_table(key) % CB


def draw_block_counts(key, part):
    base_key = jax.random.fold_in(key, 11)
    first_key, second_key, third_key = jax.random.split(base_key, 3)
    first_draw = jax.random.randint(first_key, (N_ROW, N_COL), 0, SLOTS + 1)
    second_draw = jax.random.randint(second_key, (N_ROW, N_COL), 0, SLOTS + 1)
    counts_all = jnp.maximum(first_draw * second_draw // SLOTS, SLOTS // 8)
    busiest = jax.random.randint(third_key, (), 0, N_ROW * N_COL)
    counts_all = counts_all.reshape(-1).at[busiest].set(SLOTS)
    return counts_all.reshape(N_ROW, N_COL).astype(jnp.int32)


def steps_of(key, extent, shards, low, top_value):
    gain = 1.0
    for axis_at, blocks in shards:
        steps = jax.random.uniform(jax.random.fold_in(jax.random.fold_in(key, 6), axis_at), (blocks,), jnp.float32, low / len(shards), top_value / len(shards))
        gain = gain * jnp.repeat(jnp.exp(steps), extent[axis_at] // blocks).reshape((-1,) + (1,) * (len(extent) - 1 - axis_at))
    return gain


def bell_draw(stream_key, shape, deviation, bound, cuts=(), kind=jnp.bfloat16):
    values = deviation * jax.random.normal(stream_key, shape, jnp.float32)
    if cuts:
        values = values * steps_of(stream_key, shape, cuts, -0.22, 0.18)
    return jnp.clip(values, -bound, bound).astype(kind)


def setup_inputs(seed: int = 0) -> dict:
    arg_keys = jax.random.split(jax.random.key(seed), 10)
    return {
        "features": bell_draw(arg_keys[0], (N_COL, CB * BLOCK, F), 1.0, 6.0, ((0, 8),)),
        "dst_features": bell_draw(arg_keys[1], (DST, F), 1.0, 6.0, ((0, 32),)),
        "w_self": bell_draw(arg_keys[2], (F, H), F ** -0.5, 0.5),
        "w_neigh": bell_draw(arg_keys[3], (F, H), F ** -0.5, 0.5),
        "cotangent": bell_draw(arg_keys[4], (DST, H), 1.0, 6.0, ((0, 32),)),
        "block_values": bell_draw(arg_keys[5], (N_ROW, N_COL, SLOTS, BLOCK, BLOCK), (3 * BLOCK * BLOCK * SLOTS // (10 * DST_DEV)) ** -0.5, 0.15625, ((0, 4), (1, 8))),
        "block_rows": draw_block_rows(jax.random.fold_in(arg_keys[9], 71), 0),
        "block_cols": draw_block_cols(jax.random.fold_in(arg_keys[9], 71), 0),
        "block_counts": draw_block_counts(jax.random.fold_in(arg_keys[9], 71), 0),
    }


def reference(features, dst_features, w_self, w_neigh, cotangent, block_values, block_rows, block_cols, block_counts):
    source_blocks = features.reshape(N_COL, CB, BLOCK, F)
    col_index = jnp.arange(N_COL, dtype=jnp.int32)[:, None]
    slot_index = jnp.arange(SLOTS, dtype=jnp.int32)[None, :]

    def slab_forward(group_args):
        slab_vals, slab_rows, slab_cols, slab_counts = group_args
        live_mask = (slot_index < slab_counts[:, None]).astype(jnp.float32)
        picked = source_blocks[col_index, slab_cols].astype(jnp.float32)
        products = jnp.einsum('csij,csjf->csif', slab_vals.astype(jnp.float32), picked, precision=lax.Precision.HIGHEST)
        products = products * live_mask[:, :, None, None]
        summed = jax.ops.segment_sum(products.reshape(N_COL * SLOTS, BLOCK, F), slab_rows.reshape(-1).astype(jnp.int32), num_segments=RB)
        return summed.reshape(RB * BLOCK, F)
    aggregate = lax.map(slab_forward, (block_values, block_rows, block_cols, block_counts))
    aggregate = aggregate.reshape(DST, F).astype(jnp.bfloat16)
    pre_act = jnp.dot(dst_features, w_self, preferred_element_type=jnp.float32) + jnp.dot(aggregate, w_neigh, preferred_element_type=jnp.float32)
    sigmoid_pre = jax.nn.sigmoid(pre_act)
    output = (pre_act * sigmoid_pre).astype(jnp.bfloat16)
    grad_pre = (cotangent.astype(jnp.float32) * sigmoid_pre * (1.0 + pre_act * (1.0 - sigmoid_pre))).astype(jnp.bfloat16)
    scale_factor = 1.0 / math.sqrt(DST)
    grad_w_self = jnp.dot(dst_features.T, grad_pre, preferred_element_type=jnp.float32) * scale_factor
    grad_w_neigh = jnp.dot(aggregate.T, grad_pre, preferred_element_type=jnp.float32) * scale_factor
    slab_grads = jnp.dot(grad_pre, w_neigh.T, preferred_element_type=jnp.float32).astype(jnp.bfloat16)
    slab_grads = slab_grads.reshape(N_ROW, RB, BLOCK, F)

    def slab_backward(running, group_args):
        slab_grad, slab_vals, slab_rows, slab_cols, slab_counts = group_args
        live_mask = (slot_index < slab_counts[:, None]).astype(jnp.float32)
        picked = slab_grad[slab_rows].astype(jnp.float32)
        products = jnp.einsum('csij,csif->csjf', slab_vals.astype(jnp.float32), picked, precision=lax.Precision.HIGHEST)
        products = products * live_mask[:, :, None, None]
        targets = (col_index * CB + slab_cols).reshape(-1).astype(jnp.int32)
        added = jax.ops.segment_sum(products.reshape(N_COL * SLOTS, BLOCK, F), targets, num_segments=N_COL * CB)
        return (running + added, None)
    zero_grads = jnp.zeros((N_COL * CB, BLOCK, F), jnp.float32)
    source_grad, unused = lax.scan(slab_backward, zero_grads, (slab_grads, block_values, block_rows, block_cols, block_counts))
    return (output, grad_w_self, grad_w_neigh, source_grad.reshape(N_COL, CB * BLOCK, F))
```

```python
import functools
import math

import jax
import jax.numpy as jnp
from jax import lax
from jax.experimental import pallas as pl
from jax.experimental.pallas import tpu as pltpu
from jax.sharding import PartitionSpec as P

F32 = jnp.float32
BF16 = jnp.bfloat16
VMEM = pl.BlockSpec(memory_space=pltpu.VMEM)
SMEM = pl.BlockSpec(memory_space=pltpu.SMEM)


def xor_permute(x, axis, distance):
    total = lax.axis_size(axis)
    return lax.ppermute(x, axis, [(i, i ^ distance) for i in range(total)])


def tree_sum(terms):
    while len(terms) > 1:
        terms = [terms[i] + terms[i + 1] for i in range(0, len(terms), 2)]
    return terms[0]


def forward_kernel(rows, cols, counts, values, table, mine, theirs, acc):
    slots = values.shape[2]
    pairs = mine.shape[0]
    me = lax.axis_index("col")
    acc[...] = jnp.zeros_like(acc)
    live = counts[0, 0]
    for s in range(slots):
        at = rows[0, 0, s] ^ me
        block = values[0, 0, s]
        block = jnp.where(s < live, block, jnp.zeros_like(block))
        acc[at] += jnp.dot(block, table[cols[0, 0, s]], preferred_element_type=F32)
    for p in range(pairs):
        mine[p] = acc[2 * p]
        theirs[p] = acc[2 * p + 1]


def middle_kernel(pairs, *refs):
    sums = refs[:pairs]
    dst, w_self, w_neigh, cot, output = refs[pairs : pairs + 5]
    payloads = refs[pairs + 5 : 2 * pairs + 5]
    weights = refs[2 * pairs + 5]
    z = lax.axis_index("col") // 2
    width = dst.shape[1]
    hidden = w_self.shape[1]
    agg = tree_sum([ref[...] for ref in sums]).astype(BF16)
    own = dst[...]
    pre = jnp.dot(own, w_self[...], preferred_element_type=F32) + jnp.dot(
        agg, w_neigh[...], preferred_element_type=F32
    )
    sig = jax.nn.sigmoid(pre)
    output[...] = (pre * sig).astype(BF16)
    grad_pre = (cot[...].astype(F32) * sig * (1.0 + pre * (1.0 - sig))).astype(BF16)
    grad_t = lax.dot_general(
        w_neigh[...], grad_pre, (((1,), (1,)), ((), ())), preferred_element_type=F32
    ).astype(BF16)
    nodes = (((0,), (0,)), ((), ()))
    share = weights.shape[1]
    w_both = [
        lax.dot_general(own, grad_pre, nodes, preferred_element_type=F32),
        lax.dot_general(agg, grad_pre, nodes, preferred_element_type=F32),
    ]
    for p in range(pairs):
        first = p * share
        weights[p] = w_both[first // width][first % width : first % width + share].astype(BF16)
    halves = hidden // width
    for p in range(pairs):
        payloads[p][:width] = grad_t
        chunk = weights[z ^ p]
        for h in range(halves):
            payloads[p][width + h * share : width + (h + 1) * share] = chunk[
                :, h * width : (h + 1) * width
            ]


def weight_sum_kernel(count, *refs):
    near, far, total = refs[:count], refs[count : 2 * count], refs[2 * count]
    width = total.shape[1]

    def chunk(ref):
        return ref[width:].astype(F32)

    total[...] = tree_sum([chunk(r) for r in near]) + tree_sum([chunk(r) for r in far])


def backward_kernel(pairs, groups, *refs):
    rows, cols, counts, values = refs[:4]
    near = refs[4 : 4 + pairs]
    far = refs[4 + pairs : 4 + 2 * pairs]
    own = refs[4 + 2 * pairs]
    sends = refs[5 + 2 * pairs : 4 + 2 * pairs + groups]
    table, acc = refs[4 + 2 * pairs + groups :]
    width = table.shape[1]
    slots = values.shape[2]
    share = own.shape[0]
    me = lax.axis_index("col")
    group = lax.axis_index("row")
    for p in range(pairs):
        table[2 * p] = near[p][:width]
        table[2 * p + 1] = far[p][:width]
    acc[...] = jnp.zeros_like(acc)
    live = counts[0, 0]
    for s in range(slots):
        block = values[0, 0, s]
        block = jnp.where(s < live, block, jnp.zeros_like(block))
        at = cols[0, 0, s] ^ (group * share)
        acc[at] += jnp.dot(table[rows[0, 0, s] ^ me], block, preferred_element_type=F32)
    own[...] = acc[:share]
    for g in range(1, groups):
        sends[g - 1][...] = acc[g * share : (g + 1) * share].astype(BF16)


def source_sum_kernel(groups, *refs):
    out = refs[groups]
    share, width, block = refs[0].shape
    for b in range(share):
        total = tree_sum([r[b].astype(F32) for r in refs[:groups]])
        out[b * block : (b + 1) * block, :] = total.T


def weight_join_kernel(pairs, *refs):
    chunks = refs[:pairs]
    w_self, w_neigh, table = refs[pairs : pairs + 3]
    z = lax.axis_index("col") // 2
    share = table.shape[1]
    width = chunks[0].shape[1]
    for p in range(pairs):
        for h in range(chunks[0].shape[0] // share):
            table[z ^ p, :, h * width : (h + 1) * width] = chunks[p][h * share : (h + 1) * share]
    half = pairs // 2
    for p in range(half):
        w_self[p * share : (p + 1) * share] = table[p]
        w_neigh[p * share : (p + 1) * share] = table[p + half]


def shaped(shape, dtype):
    return jax.ShapeDtypeStruct(shape, dtype)


def per_device(
    features,
    dst_features,
    w_self,
    w_neigh,
    cotangent,
    block_values,
    block_rows,
    block_cols,
    block_counts,
):
    block = block_values.shape[-1]
    width = features.shape[-1]
    hidden = w_self.shape[-1]
    local = dst_features.shape[0]
    col_total = lax.axis_size("col")
    groups = lax.axis_size("row")
    pairs = col_total // 2
    table = features.reshape(-1, block, width)
    source_blocks = table.shape[0]
    params = pltpu.CompilerParams(vmem_limit_bytes=24 * 1024 * 1024)

    mine, theirs = pl.pallas_call(
        forward_kernel,
        out_shape=[shaped((pairs, block, width), F32)] * 2,
        in_specs=[SMEM, SMEM, SMEM, VMEM, VMEM],
        out_specs=[VMEM, VMEM],
        scratch_shapes=[pltpu.VMEM((col_total, block, width), F32)],
        compiler_params=params,
        name="forward_blocks",
    )(block_rows, block_cols, block_counts, block_values, table)
    chip_sum = mine + xor_permute(theirs, "col", 1)
    sums = [chip_sum[0]] + [xor_permute(chip_sum[p], "col", 2 * p) for p in range(1, pairs)]

    share = 2 * width // pairs
    packed = shaped((width + hidden // width * share, width), BF16)
    output, *payloads = pl.pallas_call(
        functools.partial(middle_kernel, pairs),
        out_shape=[shaped((local, hidden), BF16)] + [packed] * pairs,
        in_specs=[VMEM] * (pairs + 4),
        out_specs=[VMEM] * (pairs + 1),
        scratch_shapes=[pltpu.VMEM((pairs, share, hidden), BF16)],
        compiler_params=params,
        name="dense_layer",
    )(*sums, dst_features, w_self, w_neigh, cotangent)
    near = [payloads[0]] + [xor_permute(payloads[p], "col", 2 * p) for p in range(1, pairs)]
    far = [xor_permute(x, "col", 1) for x in near]

    weight_part = pl.pallas_call(
        functools.partial(weight_sum_kernel, pairs),
        out_shape=shaped((hidden // width * share, width), F32),
        in_specs=[VMEM] * (2 * pairs),
        out_specs=VMEM,
        compiler_params=params,
        name="weight_sum",
    )(*near, *far)
    weight_terms = [weight_part] + [xor_permute(weight_part, "row", g) for g in range(1, groups)]

    source_share = source_blocks // groups
    own, *sends = pl.pallas_call(
        functools.partial(backward_kernel, pairs, groups),
        out_shape=[shaped((source_share, width, block), F32)]
        + [shaped((source_share, width, block), BF16)] * (groups - 1),
        in_specs=[SMEM, SMEM, SMEM] + [VMEM] * (1 + 2 * pairs),
        out_specs=[VMEM] * groups,
        scratch_shapes=[
            pltpu.VMEM((col_total, width, block), BF16),
            pltpu.VMEM((source_blocks, width, block), F32),
        ],
        compiler_params=params,
        name="backward_blocks",
    )(block_rows, block_cols, block_counts, block_values, *near, *far)
    source_terms = [own] + [xor_permute(x, "row", g) for g, x in enumerate(sends, 1)]

    node_total = local * groups * col_total
    weight_chunk = tree_sum(weight_terms) * (1.0 / math.sqrt(node_total))
    chunks = [weight_chunk] + [xor_permute(weight_chunk, "col", 2 * p) for p in range(1, pairs)]
    grad_self, grad_neigh = pl.pallas_call(
        functools.partial(weight_join_kernel, pairs),
        out_shape=[shaped((width, hidden), F32)] * 2,
        in_specs=[VMEM] * pairs,
        out_specs=[VMEM] * 2,
        scratch_shapes=[pltpu.VMEM((pairs, share, hidden), F32)],
        compiler_params=params,
        name="weight_join",
    )(*chunks)

    grad_source = pl.pallas_call(
        functools.partial(source_sum_kernel, groups),
        out_shape=shaped((source_share * block, width), F32),
        in_specs=[VMEM] * groups,
        out_specs=VMEM,
        compiler_params=params,
        name="source_sum",
    )(*source_terms)
    return output, grad_self, grad_neigh, grad_source.reshape(1, -1, width)


def solution(mesh):
    placed = (
        P("col", None, None),
        P(("row", "col"), None),
        P(),
        P(),
        P(("row", "col"), None),
        P("row", "col", None, None, None),
        P("row", "col", None),
        P("row", "col", None),
        P("row", "col"),
    )
    return jax.shard_map(
        per_device,
        mesh=mesh,
        in_specs=placed,
        out_specs=(P(("row", "col"), None), P(), P(), P("col", "row", None)),
        check_vma=False,
    )
```

```python
import functools
import math

import jax
import jax.numpy as jnp
from jax import lax
from jax.experimental import pallas as pl
from jax.experimental.pallas import tpu as pltpu
from jax.sharding import PartitionSpec as P

F32 = jnp.float32
BF16 = jnp.bfloat16
VMEM = pl.BlockSpec(memory_space=pltpu.VMEM)
SMEM = pl.BlockSpec(memory_space=pltpu.SMEM)
HBM = pl.BlockSpec(memory_space=pltpu.HBM)


def xor_permute(x, axis, distance):
    total = lax.axis_size(axis)
    return lax.ppermute(x, axis, [(i, i ^ distance) for i in range(total)])


def tree_sum(terms):
    while len(terms) > 1:
        terms = [terms[i] + terms[i + 1] for i in range(0, len(terms), 2)]
    return terms[0]


def forward_kernel(
    rows_in, cols_in, counts, values_in, table_in, mine, theirs, rows_out, cols_out, values, rows, cols, table, acc, sems
):
    slots = values.shape[2]
    pairs = mine.shape[0]
    parts = sems.shape[0] - 5
    step = slots // parts
    me = lax.axis_index("col")
    wanted = [(rows_in, rows), (cols_in, cols), (table_in, table)]
    passed = [(rows_in, rows_out), (cols_in, cols_out)]
    for i in range(parts):
        piece = pl.ds(i * step, step)
        wanted.append((values_in.at[0, 0, piece], values.at[0, 0, piece]))
    copies = [pltpu.make_async_copy(a, b, sems.at[i]) for i, (a, b) in enumerate(wanted + passed)]
    for copy in copies:
        copy.start()
    acc[...] = jnp.zeros_like(acc)
    for copy in copies[:3]:
        copy.wait()
    live = counts[0, 0]
    for s in range(slots):
        if s % step == 0:
            copies[3 + s // step].wait()
        at = rows[0, 0, s] ^ me
        block = values[0, 0, s]
        block = jnp.where(s < live, block, jnp.zeros_like(block))
        acc[at] += jnp.dot(block, table[cols[0, 0, s]], preferred_element_type=F32)
    for p in range(pairs):
        mine[p] = acc[2 * p]
        theirs[p] = acc[2 * p + 1]
    for copy in copies[3 + parts :]:
        copy.wait()


def middle_kernel(pairs, *refs):
    sums = refs[:pairs]
    dst, w_self, w_neigh, cot, output = refs[pairs : pairs + 5]
    payloads = refs[pairs + 5 : 2 * pairs + 5]
    weights = refs[2 * pairs + 5]
    z = lax.axis_index("col") // 2
    width = dst.shape[1]
    hidden = w_self.shape[1]
    agg = tree_sum([ref[...] for ref in sums]).astype(BF16)
    own = dst[...]
    pre = jnp.dot(own, w_self[...], preferred_element_type=F32) + jnp.dot(
        agg, w_neigh[...], preferred_element_type=F32
    )
    sig = jax.nn.sigmoid(pre)
    output[...] = (pre * sig).astype(BF16)
    grad_pre = (cot[...].astype(F32) * sig * (1.0 + pre * (1.0 - sig))).astype(BF16)
    grad_t = lax.dot_general(
        w_neigh[...], grad_pre, (((1,), (1,)), ((), ())), preferred_element_type=F32
    ).astype(BF16)
    nodes = (((0,), (0,)), ((), ()))
    share = weights.shape[1]
    w_both = [
        lax.dot_general(own, grad_pre, nodes, preferred_element_type=F32),
        lax.dot_general(agg, grad_pre, nodes, preferred_element_type=F32),
    ]
    for p in range(pairs):
        first = p * share
        weights[p] = w_both[first // width][first % width : first % width + share].astype(BF16)
    halves = hidden // width
    for p in range(pairs):
        payloads[p][:width] = grad_t
        chunk = weights[z ^ p]
        for h in range(halves):
            payloads[p][width + h * share : width + (h + 1) * share] = chunk[
                :, h * width : (h + 1) * width
            ]


def weight_sum_kernel(count, *refs):
    near, far, total = refs[:count], refs[count : 2 * count], refs[2 * count]
    width = total.shape[1]

    def chunk(ref):
        return ref[width:].astype(F32)

    total[...] = tree_sum([chunk(r) for r in near]) + tree_sum([chunk(r) for r in far])


def backward_kernel(pairs, groups, *refs):
    rows, cols, counts, values = refs[:4]
    near = refs[4 : 4 + pairs]
    far = refs[4 + pairs : 4 + 2 * pairs]
    own = refs[4 + 2 * pairs]
    sends = refs[5 + 2 * pairs : 4 + 2 * pairs + groups]
    table, acc = refs[4 + 2 * pairs + groups :]
    width = table.shape[1]
    slots = values.shape[2]
    share = own.shape[0]
    me = lax.axis_index("col")
    group = lax.axis_index("row")
    for p in range(pairs):
        table[2 * p] = near[p][:width]
        table[2 * p + 1] = far[p][:width]
    acc[...] = jnp.zeros_like(acc)
    live = counts[0, 0]
    for s in range(slots):
        block = values[0, 0, s]
        block = jnp.where(s < live, block, jnp.zeros_like(block))
        at = cols[0, 0, s] ^ (group * share)
        acc[at] += jnp.dot(table[rows[0, 0, s] ^ me], block, preferred_element_type=F32)
    own[...] = acc[:share]
    for g in range(1, groups):
        sends[g - 1][...] = acc[g * share : (g + 1) * share].astype(BF16)


def final_kernel(pairs, groups, *refs):
    chunks = refs[:pairs]
    terms = refs[pairs : pairs + groups]
    held, output, w_self, w_neigh, out, table = refs[pairs + groups :]
    output[...] = held[...]
    z = lax.axis_index("col") // 2
    share = table.shape[1]
    width = chunks[0].shape[1]
    for p in range(pairs):
        for h in range(chunks[0].shape[0] // share):
            table[z ^ p, :, h * width : (h + 1) * width] = chunks[p][h * share : (h + 1) * share]
    half = pairs // 2
    for p in range(half):
        w_self[p * share : (p + 1) * share] = table[p]
        w_neigh[p * share : (p + 1) * share] = table[p + half]
    blocks, _, block = terms[0].shape
    for b in range(blocks):
        total = tree_sum([r[b].astype(F32) for r in terms])
        out[b * block : (b + 1) * block, :] = total.T


def weight_total_kernel(scale, *refs):
    refs[-1][...] = tree_sum([r[...] for r in refs[:-1]]) * scale


def shaped(shape, dtype):
    return jax.ShapeDtypeStruct(shape, dtype)


def per_device(
    features,
    dst_features,
    w_self,
    w_neigh,
    cotangent,
    block_values,
    block_rows,
    block_cols,
    block_counts,
):
    block = block_values.shape[-1]
    width = features.shape[-1]
    hidden = w_self.shape[-1]
    local = dst_features.shape[0]
    col_total = lax.axis_size("col")
    groups = lax.axis_size("row")
    pairs = col_total // 2
    table = features.reshape(-1, block, width)
    source_blocks = table.shape[0]
    params = pltpu.CompilerParams(vmem_limit_bytes=24 * 1024 * 1024)

    inputs = (block_rows, block_cols, block_values, table)
    mine, theirs, rows, cols, values = pl.pallas_call(
        forward_kernel,
        out_shape=[shaped((pairs, block, width), F32)] * 2
        + [shaped(x.shape, x.dtype) for x in (block_rows, block_cols, block_values)],
        in_specs=[HBM, HBM, SMEM, HBM, HBM],
        out_specs=[VMEM] * 5,
        scratch_shapes=[
            pltpu.SMEM(block_rows.shape, jnp.int32),
            pltpu.SMEM(block_cols.shape, jnp.int32),
            pltpu.VMEM(table.shape, BF16),
            pltpu.VMEM((col_total, block, width), F32),
            pltpu.SemaphoreType.DMA((9,)),
        ],
        compiler_params=params,
        name="forward_blocks",
    )(
        *[pltpu.with_memory_space_constraint(x, pltpu.HBM) for x in inputs[:2]],
        block_counts,
        *[pltpu.with_memory_space_constraint(x, pltpu.HBM) for x in inputs[2:]],
    )
    chip_sum = mine + xor_permute(theirs, "col", 1)
    sums = [chip_sum[0]] + [xor_permute(chip_sum[p], "col", 2 * p) for p in range(1, pairs)]

    share = 2 * width // pairs
    packed = shaped((width + hidden // width * share, width), BF16)
    held, *payloads = pl.pallas_call(
        functools.partial(middle_kernel, pairs),
        out_shape=[shaped((local, hidden), BF16)] + [packed] * pairs,
        in_specs=[VMEM] * (pairs + 4),
        out_specs=[VMEM] * (pairs + 1),
        scratch_shapes=[pltpu.VMEM((pairs, share, hidden), BF16)],
        compiler_params=params,
        name="dense_layer",
    )(*sums, dst_features, w_self, w_neigh, cotangent)
    near = [payloads[0]] + [xor_permute(payloads[p], "col", 2 * p) for p in range(1, pairs)]
    far = [xor_permute(x, "col", 1) for x in near]

    weight_part = pl.pallas_call(
        functools.partial(weight_sum_kernel, pairs),
        out_shape=shaped((hidden // width * share, width), F32),
        in_specs=[VMEM] * (2 * pairs),
        out_specs=VMEM,
        compiler_params=params,
        name="weight_sum",
    )(*near, *far)
    weight_terms = [weight_part] + [xor_permute(weight_part, "row", g) for g in range(1, groups)]

    source_share = source_blocks // groups
    own, *sends = pl.pallas_call(
        functools.partial(backward_kernel, pairs, groups),
        out_shape=[shaped((source_share, width, block), F32)]
        + [shaped((source_share, width, block), BF16)] * (groups - 1),
        in_specs=[SMEM, SMEM, SMEM] + [VMEM] * (1 + 2 * pairs),
        out_specs=[VMEM] * groups,
        scratch_shapes=[
            pltpu.VMEM((col_total, width, block), BF16),
            pltpu.VMEM((source_blocks, width, block), F32),
        ],
        compiler_params=params,
        name="backward_blocks",
    )(rows, cols, block_counts, values, *near, *far)
    source_terms = [own] + [xor_permute(x, "row", g) for g, x in enumerate(sends, 1)]

    node_total = local * groups * col_total
    weight_chunk = pl.pallas_call(
        functools.partial(weight_total_kernel, 1.0 / math.sqrt(node_total)),
        out_shape=shaped(weight_part.shape, F32),
        in_specs=[VMEM] * groups,
        out_specs=VMEM,
        compiler_params=params,
        cost_estimate=pl.CostEstimate(flops=0, bytes_accessed=16 * 1024 * 1024, transcendentals=0),
        name="weight_total",
    )(*weight_terms)
    chunks = [weight_chunk] + [xor_permute(weight_chunk, "col", 2 * p) for p in range(1, pairs)]
    output, grad_self, grad_neigh, grad_source = pl.pallas_call(
        functools.partial(final_kernel, pairs, groups),
        out_shape=[
            shaped((local, hidden), BF16),
            shaped((width, hidden), F32),
            shaped((width, hidden), F32),
            shaped((source_share * block, width), F32),
        ],
        in_specs=[VMEM] * (pairs + groups + 1),
        out_specs=[VMEM] * 4,
        scratch_shapes=[pltpu.VMEM((pairs, share, hidden), F32)],
        compiler_params=params,
        name="join_outputs",
    )(*chunks, *source_terms, held)
    return output, grad_self, grad_neigh, grad_source.reshape(1, -1, width)


def solution(mesh):
    placed = (
        P("col", None, None),
        P(("row", "col"), None),
        P(),
        P(),
        P(("row", "col"), None),
        P("row", "col", None, None, None),
        P("row", "col", None),
        P("row", "col", None),
        P("row", "col"),
    )
    return jax.shard_map(
        per_device,
        mesh=mesh,
        in_specs=placed,
        out_specs=(P(("row", "col"), None), P(), P(), P("col", "row", None)),
        check_vma=False,
    )
```

```python
import functools
import math

import jax
import jax.numpy as jnp
from jax import lax
from jax.experimental import pallas as pl
from jax.experimental.pallas import tpu as pltpu
from jax.sharding import PartitionSpec as P

F32 = jnp.float32
BF16 = jnp.bfloat16
VMEM = pl.BlockSpec(memory_space=pltpu.VMEM)
SMEM = pl.BlockSpec(memory_space=pltpu.SMEM)
HBM = pl.BlockSpec(memory_space=pltpu.HBM)
ANY = pl.BlockSpec(memory_space=pl.ANY)


def xor_permute(x, axis, distance):
    total = lax.axis_size(axis)
    return lax.ppermute(x, axis, [(i, i ^ distance) for i in range(total)])


def tree_sum(terms):
    while len(terms) > 1:
        terms = [terms[i] + terms[i + 1] for i in range(0, len(terms), 2)]
    return terms[0]


def forward_kernel(
    rows_in, cols_in, counts, values_in, table_in, mine, theirs, rows_out, cols_out, values, rows, cols, table, acc, sems
):
    slots = values.shape[2]
    pairs = mine.shape[0]
    parts = sems.shape[0] - 5
    step = slots // parts
    me = lax.axis_index("col")
    wanted = [(rows_in, rows), (cols_in, cols), (table_in, table)]
    passed = [(rows_in, rows_out), (cols_in, cols_out)]
    for i in range(parts):
        piece = pl.ds(i * step, step)
        wanted.append((values_in.at[0, 0, piece], values.at[0, 0, piece]))
    copies = [pltpu.make_async_copy(a, b, sems.at[i]) for i, (a, b) in enumerate(wanted + passed)]
    for copy in copies:
        copy.start()
    acc[...] = jnp.zeros_like(acc)
    for copy in copies[:3]:
        copy.wait()
    live = counts[0, 0]
    for s in range(slots):
        if s % step == 0:
            copies[3 + s // step].wait()
        at = rows[0, 0, s] ^ me
        block = values[0, 0, s]
        block = jnp.where(s < live, block, jnp.zeros_like(block))
        acc[at] += jnp.dot(block, table[cols[0, 0, s]], preferred_element_type=F32)
    for p in range(pairs):
        mine[p] = acc[2 * p]
        theirs[p] = acc[2 * p + 1]
    for copy in copies[3 + parts :]:
        copy.wait()


def middle_kernel(pairs, *refs):
    sums = refs[:pairs]
    dst, w_self, w_neigh, cot, output, grad_t, grad_pre, aggregate = refs[pairs:]
    agg = tree_sum([ref[...] for ref in sums]).astype(BF16)
    aggregate[...] = agg
    pre = jnp.dot(dst[...], w_self[...], preferred_element_type=F32) + jnp.dot(
        agg, w_neigh[...], preferred_element_type=F32
    )
    sig = jax.nn.sigmoid(pre)
    output[...] = (pre * sig).astype(BF16)
    grad = (cot[...].astype(F32) * sig * (1.0 + pre * (1.0 - sig))).astype(BF16)
    grad_pre[...] = grad
    grad_t[...] = lax.dot_general(
        w_neigh[...], grad, (((1,), (1,)), ((), ())), preferred_element_type=F32
    ).astype(BF16)


def weight_kernel(dst, aggregate, grad_pre, mine, theirs):
    nodes = (((0,), (0,)), ((), ()))
    grad = grad_pre[...]
    for_self = lax.dot_general(dst[...], grad, nodes, preferred_element_type=F32)
    for_neigh = lax.dot_general(aggregate[...], grad, nodes, preferred_element_type=F32)
    first_core = lax.axis_index("col") % 2 == 0
    mine[...] = jnp.where(first_core, for_self, for_neigh)
    theirs[...] = jnp.where(first_core, for_neigh, for_self)


def weight_fold_kernel(own, received, after, total):
    total[...] = (own[...] + received[...]).astype(BF16)


def weight_total_kernel(scale, count, *refs):
    total = tree_sum([r[...].astype(F32) for r in refs[:count]]) * scale
    refs[-1][...] = total.astype(refs[-1].dtype)


def backward_kernel(pairs, groups, *refs):
    rows, cols, counts, values = refs[:4]
    near = refs[4 : 4 + pairs]
    far = refs[4 + pairs : 4 + 2 * pairs]
    own = refs[4 + 2 * pairs]
    sends = refs[5 + 2 * pairs : 4 + 2 * pairs + groups]
    table, acc = refs[4 + 2 * pairs + groups :]
    width = table.shape[1]
    slots = values.shape[2]
    share = own.shape[0]
    me = lax.axis_index("col")
    group = lax.axis_index("row")
    for p in range(pairs):
        table[2 * p] = near[p][...]
        table[2 * p + 1] = far[p][...]
    acc[...] = jnp.zeros_like(acc)
    live = counts[0, 0]
    for s in range(slots):
        block = values[0, 0, s]
        block = jnp.where(s < live, block, jnp.zeros_like(block))
        at = cols[0, 0, s] ^ (group * share)
        acc[at] += jnp.dot(table[rows[0, 0, s] ^ me], block, preferred_element_type=F32)
    own[...] = acc[:share]
    for g in range(1, groups):
        sends[g - 1][...] = acc[g * share : (g + 1) * share].astype(BF16)


def final_kernel(groups, *refs):
    weight_mine, weight_theirs, held = refs[:3]
    terms = refs[3 : 3 + groups]
    output, w_self, w_neigh, out = refs[3 + groups :]
    output[...] = held[...]
    first_core = lax.axis_index("col") % 2 == 0
    mine, theirs = weight_mine[...], weight_theirs[...]
    w_self[...] = jnp.where(first_core, mine, theirs)
    w_neigh[...] = jnp.where(first_core, theirs, mine)
    blocks, _, block = terms[0].shape
    for b in range(blocks):
        total = tree_sum([r[b].astype(F32) for r in terms])
        out[b * block : (b + 1) * block, :] = total.T


def busy(mib):
    return pl.CostEstimate(flops=0, bytes_accessed=mib * 1024 * 1024, transcendentals=0)


def shaped(shape, dtype):
    return jax.ShapeDtypeStruct(shape, dtype)


def per_device(
    features,
    dst_features,
    w_self,
    w_neigh,
    cotangent,
    block_values,
    block_rows,
    block_cols,
    block_counts,
):
    block = block_values.shape[-1]
    width = features.shape[-1]
    hidden = w_self.shape[-1]
    local = dst_features.shape[0]
    col_total = lax.axis_size("col")
    groups = lax.axis_size("row")
    pairs = col_total // 2
    table = features.reshape(-1, block, width)
    source_blocks = table.shape[0]
    params = pltpu.CompilerParams(vmem_limit_bytes=24 * 1024 * 1024)

    inputs = (block_rows, block_cols, block_values, table)
    mine, theirs, rows, cols, values = pl.pallas_call(
        forward_kernel,
        out_shape=[shaped((pairs, block, width), F32)] * 2
        + [shaped(x.shape, x.dtype) for x in (block_rows, block_cols, block_values)],
        in_specs=[HBM, HBM, SMEM, HBM, HBM],
        out_specs=[VMEM] * 5,
        scratch_shapes=[
            pltpu.SMEM(block_rows.shape, jnp.int32),
            pltpu.SMEM(block_cols.shape, jnp.int32),
            pltpu.VMEM(table.shape, BF16),
            pltpu.VMEM((col_total, block, width), F32),
            pltpu.SemaphoreType.DMA((9,)),
        ],
        compiler_params=params,
        name="forward_blocks",
    )(
        *[pltpu.with_memory_space_constraint(x, pltpu.HBM) for x in inputs[:2]],
        block_counts,
        *[pltpu.with_memory_space_constraint(x, pltpu.HBM) for x in inputs[2:]],
    )
    chip_sum = mine + xor_permute(theirs, "col", 1)
    sums = [chip_sum[0]] + [xor_permute(chip_sum[p], "col", 2 * p) for p in range(1, pairs)]

    held, grad_t, grad_pre, aggregate = pl.pallas_call(
        functools.partial(middle_kernel, pairs),
        out_shape=[
            shaped((local, hidden), BF16),
            shaped((width, local), BF16),
            shaped((local, hidden), BF16),
            shaped((local, width), BF16),
        ],
        in_specs=[VMEM] * (pairs + 4),
        out_specs=[VMEM] * 4,
        compiler_params=params,
        name="dense_layer",
    )(*sums, dst_features, w_self, w_neigh, cotangent)
    near = [grad_t] + [xor_permute(grad_t, "col", 2 * p) for p in range(1, pairs)]
    far = [xor_permute(x, "col", 1) for x in near]

    weight, weight_theirs = pl.pallas_call(
        weight_kernel,
        out_shape=[shaped((width, hidden), F32)] * 2,
        in_specs=[VMEM] * 3,
        out_specs=[VMEM] * 2,
        compiler_params=params,
        cost_estimate=busy(4),
        name="weight_partial",
    )(dst_features, aggregate, grad_pre)
    weight = pl.pallas_call(
        weight_fold_kernel,
        out_shape=shaped((width, hidden), BF16),
        in_specs=[VMEM, VMEM, ANY],
        out_specs=VMEM,
        compiler_params=params,
        name="weight_fold",
    )(weight, xor_permute(weight_theirs, "col", 1), near[-1])

    def weight_total(terms, after, dtype, scale, label):
        return pl.pallas_call(
            functools.partial(weight_total_kernel, scale, len(terms)),
            out_shape=shaped((width, hidden), dtype),
            in_specs=[VMEM] * len(terms) + [ANY] * len(after),
            out_specs=VMEM,
            compiler_params=params,
            name=label,
        )(*terms, *after)

    row_terms = [weight] + [xor_permute(weight, "row", g) for g in range(1, groups)]
    source_share = source_blocks // groups
    own, *sends = pl.pallas_call(
        functools.partial(backward_kernel, pairs, groups),
        out_shape=[shaped((source_share, width, block), F32)]
        + [shaped((source_share, width, block), BF16)] * (groups - 1),
        in_specs=[SMEM, SMEM, SMEM] + [VMEM] * (1 + 2 * pairs),
        out_specs=[VMEM] * groups,
        scratch_shapes=[
            pltpu.VMEM((col_total, width, block), BF16),
            pltpu.VMEM((source_blocks, width, block), F32),
        ],
        compiler_params=params,
        cost_estimate=busy(32),
        name="backward_blocks",
    )(rows, cols, block_counts, values, *near, *far)
    weight = weight_total(row_terms, [own], BF16, 1.0, "weight_rows")
    col_terms = [weight] + [xor_permute(weight, "col", 2 * p) for p in range(1, pairs)]
    scale = 1.0 / math.sqrt(local * groups * col_total)
    weight = weight_total(col_terms, [], F32, scale, "weight_cols")
    weight_other = xor_permute(weight, "col", 1)

    source_terms = [own] + [xor_permute(x, "row", g) for g, x in enumerate(sends, 1)]

    output, grad_self, grad_neigh, grad_source = pl.pallas_call(
        functools.partial(final_kernel, groups),
        out_shape=[
            shaped((local, hidden), BF16),
            shaped((width, hidden), F32),
            shaped((width, hidden), F32),
            shaped((source_share * block, width), F32),
        ],
        in_specs=[VMEM] * (3 + groups),
        out_specs=[VMEM] * 4,
        compiler_params=params,
        name="join_outputs",
    )(weight, weight_other, held, *source_terms)
    return output, grad_self, grad_neigh, grad_source.reshape(1, -1, width)


def solution(mesh):
    placed = (
        P("col", None, None),
        P(("row", "col"), None),
        P(),
        P(),
        P(("row", "col"), None),
        P("row", "col", None, None, None),
        P("row", "col", None),
        P("row", "col", None),
        P("row", "col"),
    )
    return jax.shard_map(
        per_device,
        mesh=mesh,
        in_specs=placed,
        out_specs=(P(("row", "col"), None), P(), P(), P("col", "row", None)),
        check_vma=False,
    )
```

```python
import functools
import math

import jax
import jax.numpy as jnp
from jax import lax
from jax.experimental import pallas as pl
from jax.experimental.pallas import tpu as pltpu
from jax.sharding import PartitionSpec as P

F32 = jnp.float32
BF16 = jnp.bfloat16
VMEM = pl.BlockSpec(memory_space=pltpu.VMEM)
SMEM = pl.BlockSpec(memory_space=pltpu.SMEM)
HBM = pl.BlockSpec(memory_space=pltpu.HBM)
ANY = pl.BlockSpec(memory_space=pl.ANY)


def xor_permute(x, axis, distance):
    total = lax.axis_size(axis)
    return lax.ppermute(x, axis, [(i, i ^ distance) for i in range(total)])


def split_permute(x, axis, even, odd):
    rows, cols = lax.axis_size("row"), lax.axis_size("col")
    pairs = []
    for r in range(rows):
        for c in range(cols):
            distance = odd if c % 2 else even
            peer = (r ^ distance, c) if axis == "row" else (r, c ^ (2 * distance))
            pairs.append((r * cols + c, peer[0] * cols + peer[1]))
    return lax.ppermute(x, ("row", "col"), pairs)


def gather_peers(whole, half, axis, count):
    seen = [split_permute(whole, axis, d, d + 1) for d in range(2, count, 2)]
    seen.append(split_permute(half, axis, 1, 1))
    return seen, [xor_permute(x, "col", 1) for x in seen]


def peer_terms(first_core, whole, seen, passed):
    def both(ref):
        return [ref[0], ref[1]]

    near, far = seen[-1][...], passed[-1][...]
    terms = [both(whole), [jnp.where(first_core, near, far), jnp.where(first_core, far, near)]]
    for near, far in zip(seen[:-1], passed[:-1]):
        near, far = both(near), both(far)
        terms.append([jnp.where(first_core, n, f) for n, f in zip(near, far)])
        terms.append([jnp.where(first_core, f, n) for n, f in zip(near, far)])
    return terms


def tree_sum(terms):
    while len(terms) > 1:
        terms = [terms[i] + terms[i + 1] for i in range(0, len(terms), 2)]
    return terms[0]


def on_first_core():
    return lax.axis_index("col") % 2 == 0


def forward_kernel(
    rows_in, cols_in, counts, values_in, table_in, mine, theirs, rows_out, cols_out, values, rows, cols, table, acc, sems
):
    slots = values.shape[2]
    pairs = mine.shape[0]
    parts = sems.shape[0] - 5
    step = slots // parts
    me = lax.axis_index("col")
    wanted = [(rows_in, rows), (cols_in, cols), (table_in, table)]
    passed = [(rows_in, rows_out), (cols_in, cols_out)]
    for i in range(parts):
        piece = pl.ds(i * step, step)
        wanted.append((values_in.at[0, 0, piece], values.at[0, 0, piece]))
    copies = [pltpu.make_async_copy(a, b, sems.at[i]) for i, (a, b) in enumerate(wanted + passed)]
    for copy in copies:
        copy.start()
    acc[...] = jnp.zeros_like(acc)
    for copy in copies[:3]:
        copy.wait()
    live = counts[0, 0]
    for s in range(slots):
        if s % step == 0:
            copies[3 + s // step].wait()
        at = rows[0, 0, s] ^ me
        block = values[0, 0, s]
        block = jnp.where(s < live, block, jnp.zeros_like(block))
        acc[at] += jnp.dot(block, table[cols[0, 0, s]], preferred_element_type=F32)
    for p in range(pairs):
        mine[p] = acc[2 * p]
        theirs[p] = acc[2 * p + 1]
    for copy in copies[3 + parts :]:
        copy.wait()


def middle_kernel(pairs, *refs):
    sums = refs[:pairs]
    dst, w_self, w_neigh, cot, output, grad_t, grad_wide, grad_pre, aggregate = refs[pairs:]
    agg = tree_sum([ref[...] for ref in sums]).astype(BF16)
    aggregate[...] = agg
    pre = jnp.dot(dst[...], w_self[...], preferred_element_type=F32) + jnp.dot(
        agg, w_neigh[...], preferred_element_type=F32
    )
    sig = jax.nn.sigmoid(pre)
    output[...] = (pre * sig).astype(BF16)
    grad = (cot[...].astype(F32) * sig * (1.0 + pre * (1.0 - sig))).astype(BF16)
    grad_pre[...] = grad
    grad_t[...] = lax.dot_general(
        w_neigh[...], grad, (((1,), (1,)), ((), ())), preferred_element_type=F32
    ).astype(BF16)
    grad_wide[...] = grad_t[...].astype(F32)


def pair_kernel(mine, theirs, pair):
    pair[0] = jnp.where(on_first_core(), mine[...], theirs[...])
    pair[1] = jnp.where(on_first_core(), theirs[...], mine[...])


def weight_kernel(dst, aggregate, grad_pre, partial):
    nodes = (((0,), (0,)), ((), ()))
    grad = grad_pre[...]
    partial[0] = lax.dot_general(dst[...], grad, nodes, preferred_element_type=F32)
    partial[1] = lax.dot_general(aggregate[...], grad, nodes, preferred_element_type=F32)


def weight_fold_kernel(mine, theirs, *rest):
    whole, half = rest[-2:]
    first = (mine[0] + theirs[0]).astype(BF16)
    second = (mine[1] + theirs[1]).astype(BF16)
    whole[0] = first
    whole[1] = second
    half[...] = jnp.where(on_first_core(), first, second)


def weight_rows_kernel(peers, *refs):
    whole, seen, passed = refs[0], refs[1 : 1 + peers], refs[1 + peers : 1 + 2 * peers]
    total, half = refs[-2:]
    terms = peer_terms(on_first_core(), whole, seen, passed)
    sums = [tree_sum([t[h].astype(F32) for t in terms]).astype(BF16) for h in range(2)]
    total[0] = sums[0]
    total[1] = sums[1]
    half[...] = jnp.where(on_first_core(), sums[0], sums[1])


def backward_kernel(peers, groups, *refs):
    rows, cols, counts, values, pair = refs[:5]
    seen, passed = refs[5 : 5 + peers], refs[5 + peers : 5 + 2 * peers]
    own, *sends = refs[5 + 2 * peers : 5 + 2 * peers + groups]
    table, acc = refs[5 + 2 * peers + groups :]
    slots = values.shape[2]
    share = own.shape[0]
    me = lax.axis_index("col") // 2 * 2
    group = lax.axis_index("row")
    for p, term in enumerate(peer_terms(on_first_core(), pair, seen, passed)):
        table[2 * p] = term[0].astype(BF16)
        table[2 * p + 1] = term[1].astype(BF16)
    acc[...] = jnp.zeros_like(acc)
    live = counts[0, 0]
    for s in range(slots):
        block = values[0, 0, s]
        block = jnp.where(s < live, block, jnp.zeros_like(block))
        at = cols[0, 0, s] ^ (group * share)
        acc[at] += jnp.dot(table[rows[0, 0, s] ^ me], block, preferred_element_type=F32)
    own[...] = acc[:share]
    for g in range(1, groups):
        sends[g - 1][...] = acc[g * share : (g + 1) * share].astype(BF16)


def final_kernel(scale, peers, groups, *refs):
    whole, seen, passed = refs[0], refs[1 : 1 + peers], refs[1 + peers : 1 + 2 * peers]
    held = refs[1 + 2 * peers]
    terms = refs[2 + 2 * peers : 2 + 2 * peers + groups]
    output, w_self, w_neigh, out = refs[2 + 2 * peers + groups :]
    output[...] = held[...]
    weights = peer_terms(on_first_core(), whole, seen, passed)
    w_self[...] = tree_sum([t[0].astype(F32) for t in weights]) * scale
    w_neigh[...] = tree_sum([t[1].astype(F32) for t in weights]) * scale
    blocks, _, block = terms[0].shape
    for b in range(blocks):
        total = tree_sum([r[b].astype(F32) for r in terms])
        out[b * block : (b + 1) * block, :] = total.T


def busy(mib):
    return pl.CostEstimate(flops=0, bytes_accessed=mib * 1024 * 1024, transcendentals=0)


def shaped(shape, dtype):
    return jax.ShapeDtypeStruct(shape, dtype)


def per_device(
    features,
    dst_features,
    w_self,
    w_neigh,
    cotangent,
    block_values,
    block_rows,
    block_cols,
    block_counts,
):
    block = block_values.shape[-1]
    width = features.shape[-1]
    hidden = w_self.shape[-1]
    local = dst_features.shape[0]
    col_total = lax.axis_size("col")
    groups = lax.axis_size("row")
    pairs = col_total // 2
    table = features.reshape(-1, block, width)
    source_blocks = table.shape[0]
    params = pltpu.CompilerParams(vmem_limit_bytes=24 * 1024 * 1024)

    inputs = (block_rows, block_cols, block_values, table)
    mine, theirs, rows, cols, values = pl.pallas_call(
        forward_kernel,
        out_shape=[shaped((pairs, block, width), F32)] * 2
        + [shaped(x.shape, x.dtype) for x in (block_rows, block_cols, block_values)],
        in_specs=[HBM, HBM, SMEM, HBM, HBM],
        out_specs=[VMEM] * 5,
        scratch_shapes=[
            pltpu.SMEM(block_rows.shape, jnp.int32),
            pltpu.SMEM(block_cols.shape, jnp.int32),
            pltpu.VMEM(table.shape, BF16),
            pltpu.VMEM((col_total, block, width), F32),
            pltpu.SemaphoreType.DMA((9,)),
        ],
        compiler_params=params,
        name="forward_blocks",
    )(
        *[pltpu.with_memory_space_constraint(x, pltpu.HBM) for x in inputs[:2]],
        block_counts,
        *[pltpu.with_memory_space_constraint(x, pltpu.HBM) for x in inputs[2:]],
    )
    chip_sum = mine + xor_permute(theirs, "col", 1)
    sums = [chip_sum[0]] + [xor_permute(chip_sum[p], "col", 2 * p) for p in range(1, pairs)]

    held, grad_t, grad_wide, grad_pre, aggregate = pl.pallas_call(
        functools.partial(middle_kernel, pairs),
        out_shape=[
            shaped((local, hidden), BF16),
            shaped((width, local), BF16),
            shaped((width, local), F32),
            shaped((local, hidden), BF16),
            shaped((local, width), BF16),
        ],
        in_specs=[VMEM] * (pairs + 4),
        out_specs=[VMEM] * 5,
        compiler_params=params,
        name="dense_layer",
    )(*sums, dst_features, w_self, w_neigh, cotangent)
    col_peers, row_peers = pairs // 2, groups // 2
    pair = pl.pallas_call(
        pair_kernel,
        out_shape=shaped((2, width, local), BF16),
        in_specs=[VMEM] * 2,
        out_specs=VMEM,
        compiler_params=params,
        name="gradient_pair",
    )(grad_t, xor_permute(grad_t, "col", 1))
    seen, passed = gather_peers(pair, grad_wide, "col", pairs)

    partial = pl.pallas_call(
        weight_kernel,
        out_shape=shaped((2, width, hidden), F32),
        in_specs=[VMEM] * 3,
        out_specs=VMEM,
        compiler_params=params,
        cost_estimate=busy(4),
        name="weight_partial",
    )(dst_features, aggregate, grad_pre)
    after = [pair]
    weight, weight_half = pl.pallas_call(
        weight_fold_kernel,
        out_shape=[shaped((2, width, hidden), BF16), shaped((width, hidden), BF16)],
        in_specs=[VMEM] * 2 + [ANY] * len(after),
        out_specs=[VMEM] * 2,
        compiler_params=params,
        name="weight_fold",
    )(partial, xor_permute(partial, "col", 1), *after)
    weight_seen, weight_passed = gather_peers(weight, weight_half, "row", groups)

    source_share = source_blocks // groups
    own, *sends = pl.pallas_call(
        functools.partial(backward_kernel, col_peers, groups),
        out_shape=[shaped((source_share, width, block), F32)]
        + [shaped((source_share, width, block), BF16)] * (groups - 1),
        in_specs=[SMEM, SMEM, SMEM] + [VMEM] * (2 + 2 * col_peers),
        out_specs=[VMEM] * groups,
        scratch_shapes=[
            pltpu.VMEM((col_total, width, block), BF16),
            pltpu.VMEM((source_blocks, width, block), F32),
        ],
        compiler_params=params,
        cost_estimate=busy(32),
        name="backward_blocks",
    )(rows, cols, block_counts, values, pair, *seen, *passed)
    after = [own]
    weight, weight_half = pl.pallas_call(
        functools.partial(weight_rows_kernel, row_peers),
        out_shape=[shaped((2, width, hidden), BF16), shaped((width, hidden), BF16)],
        in_specs=[VMEM] * (1 + 2 * row_peers) + [ANY] * len(after),
        out_specs=[VMEM] * 2,
        compiler_params=params,
        name="weight_rows",
    )(weight, *weight_seen, *weight_passed, *after)
    weight_seen, weight_passed = gather_peers(weight, weight_half, "col", pairs)
    scale = 1.0 / math.sqrt(local * groups * col_total)
    source_terms = [own] + [xor_permute(x, "row", g) for g, x in enumerate(sends, 1)]

    output, grad_self, grad_neigh, grad_source = pl.pallas_call(
        functools.partial(final_kernel, scale, col_peers, groups),
        out_shape=[
            shaped((local, hidden), BF16),
            shaped((width, hidden), F32),
            shaped((width, hidden), F32),
            shaped((source_share * block, width), F32),
        ],
        in_specs=[VMEM] * (2 + 2 * col_peers + groups),
        out_specs=[VMEM] * 4,
        compiler_params=params,
        name="join_outputs",
    )(weight, *weight_seen, *weight_passed, held, *source_terms)
    return output, grad_self, grad_neigh, grad_source.reshape(1, -1, width)


def solution(mesh):
    placed = (
        P("col", None, None),
        P(("row", "col"), None),
        P(),
        P(),
        P(("row", "col"), None),
        P("row", "col", None, None, None),
        P("row", "col", None),
        P("row", "col", None),
        P("row", "col"),
    )
    return jax.shard_map(
        per_device,
        mesh=mesh,
        in_specs=placed,
        out_specs=(P(("row", "col"), None), P(), P(), P("col", "row", None)),
        check_vma=False,
    )
```

```python
import functools
import math

import jax
import jax.numpy as jnp
from jax import lax
from jax.experimental import pallas as pl
from jax.experimental.pallas import tpu as pltpu
from jax.sharding import PartitionSpec as P

F32 = jnp.float32
BF16 = jnp.bfloat16
VMEM = pl.BlockSpec(memory_space=pltpu.VMEM)
SMEM = pl.BlockSpec(memory_space=pltpu.SMEM)
HBM = pl.BlockSpec(memory_space=pltpu.HBM)
ANY = pl.BlockSpec(memory_space=pl.ANY)


def xor_permute(x, axis, distance):
    total = lax.axis_size(axis)
    return lax.ppermute(x, axis, [(i, i ^ distance) for i in range(total)])


def split_permute(x, axis, even, odd):
    rows, cols = lax.axis_size("row"), lax.axis_size("col")
    pairs = []
    for r in range(rows):
        for c in range(cols):
            distance = odd if c % 2 else even
            peer = (r ^ distance, c) if axis == "row" else (r, c ^ (2 * distance))
            pairs.append((r * cols + c, peer[0] * cols + peer[1]))
    return lax.ppermute(x, ("row", "col"), pairs)


def gather_peers(whole, half, axis, count):
    seen = [split_permute(whole, axis, d, d + 1) for d in range(2, count, 2)]
    seen.append(split_permute(half, axis, 1, 1))
    return seen, [xor_permute(x, "col", 1) for x in seen]


def peer_terms(first_core, whole, seen, passed):
    def both(ref):
        return [ref[0], ref[1]]

    near, far = seen[-1][:, : whole.shape[2]], passed[-1][:, : whole.shape[2]]
    terms = [both(whole), [jnp.where(first_core, near, far), jnp.where(first_core, far, near)]]
    for near, far in zip(seen[:-1], passed[:-1]):
        near, far = both(near), both(far)
        terms.append([jnp.where(first_core, n, f) for n, f in zip(near, far)])
        terms.append([jnp.where(first_core, f, n) for n, f in zip(near, far)])
    return terms


def tree_sum(terms):
    while len(terms) > 1:
        terms = [terms[i] + terms[i + 1] for i in range(0, len(terms), 2)]
    return terms[0]


def on_first_core():
    return lax.axis_index("col") % 2 == 0


def forward_kernel(
    rows_in, cols_in, counts, values_in, table_in, mine, theirs, rows_out, cols_out, values, rows, cols, table, acc, sems
):
    slots = values.shape[2]
    pairs = mine.shape[0]
    parts = sems.shape[0] - 5
    step = slots // parts
    me = lax.axis_index("col")
    wanted = [(rows_in, rows), (cols_in, cols), (table_in, table)]
    passed = [(rows_in, rows_out), (cols_in, cols_out)]
    for i in range(parts):
        piece = pl.ds(i * step, step)
        wanted.append((values_in.at[0, 0, piece], values.at[0, 0, piece]))
    copies = [pltpu.make_async_copy(a, b, sems.at[i]) for i, (a, b) in enumerate(wanted + passed)]
    for copy in copies:
        copy.start()
    acc[...] = jnp.zeros_like(acc)
    for copy in copies[:3]:
        copy.wait()
    live = counts[0, 0]
    for s in range(slots):
        if s % step == 0:
            copies[3 + s // step].wait()
        at = rows[0, 0, s] ^ me
        block = values[0, 0, s]
        block = jnp.where(s < live, block, jnp.zeros_like(block))
        acc[at] += jnp.dot(block, table[cols[0, 0, s]], preferred_element_type=F32)
    for p in range(pairs):
        mine[p] = acc[2 * p]
        theirs[p] = acc[2 * p + 1]
    for copy in copies[3 + parts :]:
        copy.wait()


def middle_kernel(pairs, *refs):
    sums = refs[:pairs]
    dst, w_self, w_neigh, cot, output, grad_t, grad_wide, partial = refs[pairs:]
    agg = tree_sum([ref[...] for ref in sums]).astype(BF16)
    pre = jnp.dot(dst[...], w_self[...], preferred_element_type=F32) + jnp.dot(
        agg, w_neigh[...], preferred_element_type=F32
    )
    sig = jax.nn.sigmoid(pre)
    output[...] = (pre * sig).astype(BF16)
    grad = (cot[...].astype(F32) * sig * (1.0 + pre * (1.0 - sig))).astype(BF16)
    grad_t[...] = lax.dot_general(
        w_neigh[...], grad, (((1,), (1,)), ((), ())), preferred_element_type=F32
    ).astype(BF16)
    grad_wide[...] = jnp.concatenate([grad_t[...], jnp.zeros_like(grad_t)], axis=1).astype(F32)
    nodes = (((0,), (0,)), ((), ()))
    partial[0] = lax.dot_general(dst[...], grad, nodes, preferred_element_type=F32)
    partial[1] = lax.dot_general(agg, grad, nodes, preferred_element_type=F32)


def pair_kernel(mine, theirs, pair):
    pair[0] = jnp.where(on_first_core(), mine[...], theirs[...])
    pair[1] = jnp.where(on_first_core(), theirs[...], mine[...])


def weight_fold_kernel(mine, theirs, *rest):
    whole, half = rest[-2:]
    first = (mine[0] + theirs[0]).astype(BF16)
    second = (mine[1] + theirs[1]).astype(BF16)
    whole[0] = first
    whole[1] = second
    half[...] = jnp.where(on_first_core(), first, second)


def weight_rows_kernel(peers, *refs):
    whole, seen, passed = refs[0], refs[1 : 1 + peers], refs[1 + peers : 1 + 2 * peers]
    total, half = refs[-2:]
    terms = peer_terms(on_first_core(), whole, seen, passed)
    sums = [tree_sum([t[h].astype(F32) for t in terms]).astype(BF16) for h in range(2)]
    total[0] = sums[0]
    total[1] = sums[1]
    half[...] = jnp.where(on_first_core(), sums[0], sums[1])


def backward_kernel(peers, groups, *refs):
    rows, cols, counts, values, pair = refs[:5]
    seen, passed = refs[5 : 5 + peers], refs[5 + peers : 5 + 2 * peers]
    own, *sends = refs[5 + 2 * peers : 5 + 2 * peers + groups]
    table, acc = refs[5 + 2 * peers + groups :]
    slots = values.shape[2]
    share = own.shape[0]
    me = lax.axis_index("col") // 2 * 2
    group = lax.axis_index("row")
    for p, term in enumerate(peer_terms(on_first_core(), pair, seen, passed)):
        table[2 * p] = term[0].astype(BF16)
        table[2 * p + 1] = term[1].astype(BF16)
    acc[...] = jnp.zeros_like(acc)
    live = counts[0, 0]
    for s in range(slots):
        block = values[0, 0, s]
        block = jnp.where(s < live, block, jnp.zeros_like(block))
        at = cols[0, 0, s] ^ (group * share)
        acc[at] += jnp.dot(table[rows[0, 0, s] ^ me], block, preferred_element_type=F32)
    own[...] = acc[:share]
    for g in range(1, groups):
        sends[g - 1][...] = acc[g * share : (g + 1) * share].astype(BF16)


def final_kernel(scale, peers, groups, *refs):
    whole, seen, passed = refs[0], refs[1 : 1 + peers], refs[1 + peers : 1 + 2 * peers]
    held = refs[1 + 2 * peers]
    terms = refs[2 + 2 * peers : 2 + 2 * peers + groups]
    output, w_self, w_neigh, out = refs[2 + 2 * peers + groups :]
    output[...] = held[...]
    weights = peer_terms(on_first_core(), whole, seen, passed)
    w_self[...] = tree_sum([t[0].astype(F32) for t in weights]) * scale
    w_neigh[...] = tree_sum([t[1].astype(F32) for t in weights]) * scale
    blocks, _, block = terms[0].shape
    for b in range(blocks):
        total = tree_sum([r[b].astype(F32) for r in terms])
        out[b * block : (b + 1) * block, :] = total.T


def busy(mib):
    return pl.CostEstimate(flops=0, bytes_accessed=mib * 1024 * 1024, transcendentals=0)


def shaped(shape, dtype):
    return jax.ShapeDtypeStruct(shape, dtype)


def per_device(
    features,
    dst_features,
    w_self,
    w_neigh,
    cotangent,
    block_values,
    block_rows,
    block_cols,
    block_counts,
):
    block = block_values.shape[-1]
    width = features.shape[-1]
    hidden = w_self.shape[-1]
    local = dst_features.shape[0]
    col_total = lax.axis_size("col")
    groups = lax.axis_size("row")
    pairs = col_total // 2
    table = features.reshape(-1, block, width)
    source_blocks = table.shape[0]
    params = pltpu.CompilerParams(vmem_limit_bytes=24 * 1024 * 1024)

    inputs = (block_rows, block_cols, block_values, table)
    mine, theirs, rows, cols, values = pl.pallas_call(
        forward_kernel,
        out_shape=[shaped((pairs, block, width), F32)] * 2
        + [shaped(x.shape, x.dtype) for x in (block_rows, block_cols, block_values)],
        in_specs=[HBM, HBM, SMEM, HBM, HBM],
        out_specs=[VMEM] * 5,
        scratch_shapes=[
            pltpu.SMEM(block_rows.shape, jnp.int32),
            pltpu.SMEM(block_cols.shape, jnp.int32),
            pltpu.VMEM(table.shape, BF16),
            pltpu.VMEM((col_total, block, width), F32),
            pltpu.SemaphoreType.DMA((9,)),
        ],
        compiler_params=params,
        name="forward_blocks",
    )(
        *[pltpu.with_memory_space_constraint(x, pltpu.HBM) for x in inputs[:2]],
        block_counts,
        *[pltpu.with_memory_space_constraint(x, pltpu.HBM) for x in inputs[2:]],
    )
    chip_sum = mine + xor_permute(theirs, "col", 1)
    sums = [chip_sum[0]] + [xor_permute(chip_sum[p], "col", 2 * p) for p in range(1, pairs)]

    held, grad_t, grad_wide, partial = pl.pallas_call(
        functools.partial(middle_kernel, pairs),
        out_shape=[
            shaped((local, hidden), BF16),
            shaped((width, local), BF16),
            shaped((width, 2 * local), F32),
            shaped((2, width, hidden), F32),
        ],
        in_specs=[VMEM] * (pairs + 4),
        out_specs=[VMEM] * 4,
        compiler_params=params,
        name="dense_layer",
    )(*sums, dst_features, w_self, w_neigh, cotangent)
    col_peers, row_peers = pairs // 2, groups // 2
    pair = pl.pallas_call(
        pair_kernel,
        out_shape=shaped((2, width, local), BF16),
        in_specs=[VMEM] * 2,
        out_specs=VMEM,
        compiler_params=params,
        name="gradient_pair",
    )(grad_t, xor_permute(grad_t, "col", 1))
    seen, passed = gather_peers(pair, grad_wide, "col", pairs)

    after = [pair]
    weight, weight_half = pl.pallas_call(
        weight_fold_kernel,
        out_shape=[shaped((2, width, hidden), BF16), shaped((width, hidden), BF16)],
        in_specs=[VMEM] * 2 + [ANY] * len(after),
        out_specs=[VMEM] * 2,
        compiler_params=params,
        name="weight_fold",
    )(partial, xor_permute(partial, "col", 1), *after)
    weight_seen, weight_passed = gather_peers(weight, weight_half, "row", groups)

    source_share = source_blocks // groups
    own, *sends = pl.pallas_call(
        functools.partial(backward_kernel, col_peers, groups),
        out_shape=[shaped((source_share, width, block), F32)]
        + [shaped((source_share, width, block), BF16)] * (groups - 1),
        in_specs=[SMEM, SMEM, SMEM] + [VMEM] * (2 + 2 * col_peers),
        out_specs=[VMEM] * groups,
        scratch_shapes=[
            pltpu.VMEM((col_total, width, block), BF16),
            pltpu.VMEM((source_blocks, width, block), F32),
        ],
        compiler_params=params,
        cost_estimate=busy(32),
        name="backward_blocks",
    )(rows, cols, block_counts, values, pair, *seen, *passed)
    after = [own]
    weight, weight_half = pl.pallas_call(
        functools.partial(weight_rows_kernel, row_peers),
        out_shape=[shaped((2, width, hidden), BF16), shaped((width, hidden), BF16)],
        in_specs=[VMEM] * (1 + 2 * row_peers) + [ANY] * len(after),
        out_specs=[VMEM] * 2,
        compiler_params=params,
        name="weight_rows",
    )(weight, *weight_seen, *weight_passed, *after)
    weight_seen, weight_passed = gather_peers(weight, weight_half, "col", pairs)
    scale = 1.0 / math.sqrt(local * groups * col_total)
    source_terms = [own] + [xor_permute(x, "row", g) for g, x in enumerate(sends, 1)]

    output, grad_self, grad_neigh, grad_source = pl.pallas_call(
        functools.partial(final_kernel, scale, col_peers, groups),
        out_shape=[
            shaped((local, hidden), BF16),
            shaped((width, hidden), F32),
            shaped((width, hidden), F32),
            shaped((source_share * block, width), F32),
        ],
        in_specs=[VMEM] * (2 + 2 * col_peers + groups),
        out_specs=[VMEM] * 4,
        compiler_params=params,
        name="join_outputs",
    )(weight, *weight_seen, *weight_passed, held, *source_terms)
    return output, grad_self, grad_neigh, grad_source.reshape(1, -1, width)


def solution(mesh):
    placed = (
        P("col", None, None),
        P(("row", "col"), None),
        P(),
        P(),
        P(("row", "col"), None),
        P("row", "col", None, None, None),
        P("row", "col", None),
        P("row", "col", None),
        P("row", "col"),
    )
    return jax.shard_map(
        per_device,
        mesh=mesh,
        in_specs=placed,
        out_specs=(P(("row", "col"), None), P(), P(), P("col", "row", None)),
        check_vma=False,
    )
```

```python
import functools
import math

import jax
import jax.numpy as jnp
from jax import lax
from jax.experimental import pallas as pl
from jax.experimental.pallas import tpu as pltpu
from jax.sharding import PartitionSpec as P

F32 = jnp.float32
BF16 = jnp.bfloat16
VMEM = pl.BlockSpec(memory_space=pltpu.VMEM)
SMEM = pl.BlockSpec(memory_space=pltpu.SMEM)
HBM = pl.BlockSpec(memory_space=pltpu.HBM)
ANY = pl.BlockSpec(memory_space=pl.ANY)


def xor_permute(x, axis, distance):
    total = lax.axis_size(axis)
    return lax.ppermute(x, axis, [(i, i ^ distance) for i in range(total)])


def split_permute(x, axis, even, odd):
    rows, cols = lax.axis_size("row"), lax.axis_size("col")
    pairs = []
    for r in range(rows):
        for c in range(cols):
            distance = odd if c % 2 else even
            peer = (r ^ distance, c) if axis == "row" else (r, c ^ (2 * distance))
            pairs.append((r * cols + c, peer[0] * cols + peer[1]))
    return lax.ppermute(x, ("row", "col"), pairs)


def gather_peers(whole, half, axis, count):
    seen = [split_permute(whole, axis, d, d + 1) for d in range(2, count, 2)]
    seen.append(split_permute(half, axis, 1, 1))
    return seen, [xor_permute(x, "col", 1) for x in seen]


def peer_terms(first_core, whole, seen, passed):
    def both(ref):
        return [ref[0], ref[1]]

    near, far = seen[-1][:, : whole.shape[2]], passed[-1][:, : whole.shape[2]]
    terms = [both(whole), [jnp.where(first_core, near, far), jnp.where(first_core, far, near)]]
    for near, far in zip(seen[:-1], passed[:-1]):
        near, far = both(near), both(far)
        terms.append([jnp.where(first_core, n, f) for n, f in zip(near, far)])
        terms.append([jnp.where(first_core, f, n) for n, f in zip(near, far)])
    return terms


def tree_sum(terms):
    while len(terms) > 1:
        terms = [terms[i] + terms[i + 1] for i in range(0, len(terms), 2)]
    return terms[0]


def on_first_core():
    return lax.axis_index("col") % 2 == 0


def forward_kernel(
    rows_in, cols_in, counts, values_in, table_in, mine, theirs, rows_out, cols_out, values, rows, cols, table, acc, sems
):
    slots = values.shape[2]
    pairs = mine.shape[0]
    parts = sems.shape[0] - 5
    step = slots // parts
    me = lax.axis_index("col")
    wanted = [(rows_in, rows), (cols_in, cols), (table_in, table)]
    passed = [(rows_in, rows_out), (cols_in, cols_out)]
    for i in range(parts):
        piece = pl.ds(i * step, step)
        wanted.append((values_in.at[0, 0, piece], values.at[0, 0, piece]))
    copies = [pltpu.make_async_copy(a, b, sems.at[i]) for i, (a, b) in enumerate(wanted + passed)]
    for copy in copies:
        copy.start()
    acc[...] = jnp.zeros_like(acc)
    for copy in copies[:3]:
        copy.wait()
    live = counts[0, 0]
    for s in range(slots):
        if s % step == 0:
            copies[3 + s // step].wait()
        at = rows[0, 0, s] ^ me
        block = values[0, 0, s]
        block = jnp.where(s < live, block, jnp.zeros_like(block))
        acc[at] += jnp.dot(block, table[cols[0, 0, s]], preferred_element_type=F32)
    for p in range(pairs):
        mine[p] = acc[2 * p]
        theirs[p] = acc[2 * p + 1]
    for copy in copies[3 + parts :]:
        copy.wait()


def middle_kernel(pairs, *refs):
    sums = refs[:pairs]
    dst, w_self, w_neigh, cot, output, grad_t, grad_wide, partial = refs[pairs:]
    agg = tree_sum([ref[...].astype(F32) for ref in sums]).astype(BF16)
    pre = jnp.dot(dst[...], w_self[...], preferred_element_type=F32) + jnp.dot(
        agg, w_neigh[...], preferred_element_type=F32
    )
    sig = jax.nn.sigmoid(pre)
    output[...] = (pre * sig).astype(BF16)
    grad = (cot[...].astype(F32) * sig * (1.0 + pre * (1.0 - sig))).astype(BF16)
    grad_t[...] = lax.dot_general(
        w_neigh[...], grad, (((1,), (1,)), ((), ())), preferred_element_type=F32
    ).astype(BF16)
    grad_wide[...] = jnp.concatenate([grad_t[...], jnp.zeros_like(grad_t)], axis=1).astype(F32)
    nodes = (((0,), (0,)), ((), ()))
    partial[0] = lax.dot_general(dst[...], grad, nodes, preferred_element_type=F32)
    partial[1] = lax.dot_general(agg, grad, nodes, preferred_element_type=F32)


def pair_kernel(mine, theirs, pair):
    pair[0] = jnp.where(on_first_core(), mine[...], theirs[...])
    pair[1] = jnp.where(on_first_core(), theirs[...], mine[...])


def weight_fold_kernel(mine, theirs, *rest):
    whole, half = rest[-2:]
    first = (mine[0] + theirs[0]).astype(BF16)
    second = (mine[1] + theirs[1]).astype(BF16)
    whole[0] = first
    whole[1] = second
    half[...] = jnp.where(on_first_core(), first, second)


def weight_rows_kernel(peers, *refs):
    whole, seen, passed = refs[0], refs[1 : 1 + peers], refs[1 + peers : 1 + 2 * peers]
    total, half = refs[-2:]
    terms = peer_terms(on_first_core(), whole, seen, passed)
    sums = [tree_sum([t[h].astype(F32) for t in terms]).astype(BF16) for h in range(2)]
    total[0] = sums[0]
    total[1] = sums[1]
    half[...] = jnp.where(on_first_core(), sums[0], sums[1])


def backward_kernel(peers, groups, *refs):
    rows, cols, counts, values, pair = refs[:5]
    seen, passed = refs[5 : 5 + peers], refs[5 + peers : 5 + 2 * peers]
    own, *sends = refs[5 + 2 * peers : 5 + 2 * peers + groups]
    table, acc = refs[5 + 2 * peers + groups :]
    slots = values.shape[2]
    share = own.shape[0]
    me = lax.axis_index("col") // 2 * 2
    group = lax.axis_index("row")
    for p, term in enumerate(peer_terms(on_first_core(), pair, seen, passed)):
        table[2 * p] = term[0].astype(BF16)
        table[2 * p + 1] = term[1].astype(BF16)
    acc[...] = jnp.zeros_like(acc)
    live = counts[0, 0]
    for s in range(slots):
        block = values[0, 0, s]
        block = jnp.where(s < live, block, jnp.zeros_like(block))
        at = cols[0, 0, s] ^ (group * share)
        acc[at] += jnp.dot(table[rows[0, 0, s] ^ me], block, preferred_element_type=F32)
    own[...] = acc[:share]
    for g in range(1, groups):
        sends[g - 1][...] = acc[g * share : (g + 1) * share].astype(BF16)


def final_kernel(scale, peers, groups, *refs):
    whole, seen, passed = refs[0], refs[1 : 1 + peers], refs[1 + peers : 1 + 2 * peers]
    held = refs[1 + 2 * peers]
    terms = refs[2 + 2 * peers : 2 + 2 * peers + groups]
    output, w_self, w_neigh, out = refs[2 + 2 * peers + groups :]
    output[...] = held[...]
    weights = peer_terms(on_first_core(), whole, seen, passed)
    w_self[...] = tree_sum([t[0].astype(F32) for t in weights]) * scale
    w_neigh[...] = tree_sum([t[1].astype(F32) for t in weights]) * scale
    blocks, _, block = terms[0].shape
    for b in range(blocks):
        total = tree_sum([r[b].astype(F32) for r in terms])
        out[b * block : (b + 1) * block, :] = total.T


def busy(mib):
    return pl.CostEstimate(flops=0, bytes_accessed=mib * 1024 * 1024, transcendentals=0)


def shaped(shape, dtype):
    return jax.ShapeDtypeStruct(shape, dtype)


def per_device(
    features,
    dst_features,
    w_self,
    w_neigh,
    cotangent,
    block_values,
    block_rows,
    block_cols,
    block_counts,
):
    block = block_values.shape[-1]
    width = features.shape[-1]
    hidden = w_self.shape[-1]
    local = dst_features.shape[0]
    col_total = lax.axis_size("col")
    groups = lax.axis_size("row")
    pairs = col_total // 2
    table = features.reshape(-1, block, width)
    source_blocks = table.shape[0]
    params = pltpu.CompilerParams(vmem_limit_bytes=24 * 1024 * 1024)

    inputs = (block_rows, block_cols, block_values, table)
    mine, theirs, rows, cols, values = pl.pallas_call(
        forward_kernel,
        out_shape=[shaped((pairs, block, width), F32)] * 2
        + [shaped(x.shape, x.dtype) for x in (block_rows, block_cols, block_values)],
        in_specs=[HBM, HBM, SMEM, HBM, HBM],
        out_specs=[VMEM] * 5,
        scratch_shapes=[
            pltpu.SMEM(block_rows.shape, jnp.int32),
            pltpu.SMEM(block_cols.shape, jnp.int32),
            pltpu.VMEM(table.shape, BF16),
            pltpu.VMEM((col_total, block, width), F32),
            pltpu.SemaphoreType.DMA((9,)),
        ],
        compiler_params=params,
        name="forward_blocks",
    )(
        *[pltpu.with_memory_space_constraint(x, pltpu.HBM) for x in inputs[:2]],
        block_counts,
        *[pltpu.with_memory_space_constraint(x, pltpu.HBM) for x in inputs[2:]],
    )
    chip_sum = mine + xor_permute(theirs, "col", 1)
    sums = [chip_sum[0]] + [xor_permute(chip_sum[p].astype(BF16), "col", 2 * p) for p in range(1, pairs)]

    held, grad_t, grad_wide, partial = pl.pallas_call(
        functools.partial(middle_kernel, pairs),
        out_shape=[
            shaped((local, hidden), BF16),
            shaped((width, local), BF16),
            shaped((width, 2 * local), F32),
            shaped((2, width, hidden), F32),
        ],
        in_specs=[VMEM] * (pairs + 4),
        out_specs=[VMEM] * 4,
        compiler_params=params,
        name="dense_layer",
    )(*sums, dst_features, w_self, w_neigh, cotangent)
    col_peers, row_peers = pairs // 2, groups // 2
    pair = pl.pallas_call(
        pair_kernel,
        out_shape=shaped((2, width, local), BF16),
        in_specs=[VMEM] * 2,
        out_specs=VMEM,
        compiler_params=params,
        name="gradient_pair",
    )(grad_t, xor_permute(grad_t, "col", 1))
    seen, passed = gather_peers(pair, grad_wide, "col", pairs)

    after = [pair]
    weight, weight_half = pl.pallas_call(
        weight_fold_kernel,
        out_shape=[shaped((2, width, hidden), BF16), shaped((width, hidden), BF16)],
        in_specs=[VMEM] * 2 + [ANY] * len(after),
        out_specs=[VMEM] * 2,
        compiler_params=params,
        name="weight_fold",
    )(partial, xor_permute(partial, "col", 1), *after)
    weight_seen, weight_passed = gather_peers(weight, weight_half, "row", groups)

    source_share = source_blocks // groups
    own, *sends = pl.pallas_call(
        functools.partial(backward_kernel, col_peers, groups),
        out_shape=[shaped((source_share, width, block), F32)]
        + [shaped((source_share, width, block), BF16)] * (groups - 1),
        in_specs=[SMEM, SMEM, SMEM] + [VMEM] * (2 + 2 * col_peers),
        out_specs=[VMEM] * groups,
        scratch_shapes=[
            pltpu.VMEM((col_total, width, block), BF16),
            pltpu.VMEM((source_blocks, width, block), F32),
        ],
        compiler_params=params,
        cost_estimate=busy(32),
        name="backward_blocks",
    )(rows, cols, block_counts, values, pair, *seen, *passed)
    after = passed
    weight, weight_half = pl.pallas_call(
        functools.partial(weight_rows_kernel, row_peers),
        out_shape=[shaped((2, width, hidden), BF16), shaped((width, hidden), BF16)],
        in_specs=[VMEM] * (1 + 2 * row_peers) + [ANY] * len(after),
        out_specs=[VMEM] * 2,
        compiler_params=params,
        name="weight_rows",
    )(weight, *weight_seen, *weight_passed, *after)
    weight_seen, weight_passed = gather_peers(weight, weight_half, "col", pairs)
    scale = 1.0 / math.sqrt(local * groups * col_total)
    source_terms = [own] + [xor_permute(x, "row", g) for g, x in enumerate(sends, 1)]

    output, grad_self, grad_neigh, grad_source = pl.pallas_call(
        functools.partial(final_kernel, scale, col_peers, groups),
        out_shape=[
            shaped((local, hidden), BF16),
            shaped((width, hidden), F32),
            shaped((width, hidden), F32),
            shaped((source_share * block, width), F32),
        ],
        in_specs=[VMEM] * (2 + 2 * col_peers + groups),
        out_specs=[VMEM] * 4,
        compiler_params=params,
        name="join_outputs",
    )(weight, *weight_seen, *weight_passed, held, *source_terms)
    return output, grad_self, grad_neigh, grad_source.reshape(1, -1, width)


def solution(mesh):
    placed = (
        P("col", None, None),
        P(("row", "col"), None),
        P(),
        P(),
        P(("row", "col"), None),
        P("row", "col", None, None, None),
        P("row", "col", None),
        P("row", "col", None),
        P("row", "col"),
    )
    return jax.shard_map(
        per_device,
        mesh=mesh,
        in_specs=placed,
        out_specs=(P(("row", "col"), None), P(), P(), P("col", "row", None)),
        check_vma=False,
    )
```

```python
import functools
import math

import jax
import jax.numpy as jnp
from jax import lax
from jax.experimental import pallas as pl
from jax.experimental.pallas import tpu as pltpu
from jax.sharding import PartitionSpec as P

F32 = jnp.float32
BF16 = jnp.bfloat16
VMEM = pl.BlockSpec(memory_space=pltpu.VMEM)
SMEM = pl.BlockSpec(memory_space=pltpu.SMEM)
HBM = pl.BlockSpec(memory_space=pltpu.HBM)
ANY = pl.BlockSpec(memory_space=pl.ANY)


def xor_permute(x, axis, distance):
    total = lax.axis_size(axis)
    return lax.ppermute(x, axis, [(i, i ^ distance) for i in range(total)])


def split_permute(x, axis, even, odd):
    rows, cols = lax.axis_size("row"), lax.axis_size("col")
    pairs = []
    for r in range(rows):
        for c in range(cols):
            distance = odd if c % 2 else even
            peer = (r ^ distance, c) if axis == "row" else (r, c ^ (2 * distance))
            pairs.append((r * cols + c, peer[0] * cols + peer[1]))
    return lax.ppermute(x, ("row", "col"), pairs)


def gather_peers(whole, half, axis, count):
    seen = [split_permute(whole, axis, d, d + 1) for d in range(2, count, 2)]
    seen.append(split_permute(half, axis, 1, 1))
    return seen, [xor_permute(x, "col", 1) for x in seen]


def peer_terms(first_core, whole, seen, passed):
    def both(ref):
        return [ref[0], ref[1]]

    near, far = seen[-1][:, : whole.shape[2]], passed[-1][:, : whole.shape[2]]
    terms = [both(whole), [jnp.where(first_core, near, far), jnp.where(first_core, far, near)]]
    for near, far in zip(seen[:-1], passed[:-1]):
        near, far = both(near), both(far)
        terms.append([jnp.where(first_core, n, f) for n, f in zip(near, far)])
        terms.append([jnp.where(first_core, f, n) for n, f in zip(near, far)])
    return terms


def tree_sum(terms):
    while len(terms) > 1:
        terms = [terms[i] + terms[i + 1] for i in range(0, len(terms), 2)]
    return terms[0]


def on_first_core():
    return lax.axis_index("col") % 2 == 0


def forward_kernel(
    rows_in, cols_in, counts, values_in, table_in, mine, theirs, rows_out, cols_out, values, rows, cols, table, acc, sems
):
    slots = values.shape[2]
    pairs = mine.shape[0]
    parts = sems.shape[0] - 5
    step = slots // parts
    me = lax.axis_index("col")
    wanted = [(rows_in, rows), (cols_in, cols), (table_in, table)]
    passed = [(rows_in, rows_out), (cols_in, cols_out)]
    for i in range(parts):
        piece = pl.ds(i * step, step)
        wanted.append((values_in.at[0, 0, piece], values.at[0, 0, piece]))
    copies = [pltpu.make_async_copy(a, b, sems.at[i]) for i, (a, b) in enumerate(wanted + passed)]
    for copy in copies:
        copy.start()
    acc[...] = jnp.zeros_like(acc)
    for copy in copies[:3]:
        copy.wait()
    live = counts[0, 0]
    for s in range(slots):
        if s % step == 0:
            copies[3 + s // step].wait()
        at = rows[0, 0, s] ^ me
        block = values[0, 0, s]
        block = jnp.where(s < live, block, jnp.zeros_like(block))
        acc[at] += jnp.dot(block, table[cols[0, 0, s]], preferred_element_type=F32)
    for p in range(pairs):
        mine[p] = acc[2 * p]
        theirs[p] = acc[2 * p + 1]
    for copy in copies[3 + parts :]:
        copy.wait()


def middle_kernel(pairs, *refs):
    sums = refs[:pairs]
    dst, w_self, w_neigh, cot, output, grad_t, grad_wide, partial = refs[pairs:]
    agg = tree_sum([ref[...].astype(F32) for ref in sums]).astype(BF16)
    pre = jnp.dot(dst[...], w_self[...], preferred_element_type=F32) + jnp.dot(
        agg, w_neigh[...], preferred_element_type=F32
    )
    sig = jax.nn.sigmoid(pre)
    output[...] = (pre * sig).astype(BF16)
    grad = (cot[...].astype(F32) * sig * (1.0 + pre * (1.0 - sig))).astype(BF16)
    grad_t[...] = lax.dot_general(
        w_neigh[...], grad, (((1,), (1,)), ((), ())), preferred_element_type=F32
    ).astype(BF16)
    grad_wide[...] = jnp.concatenate([grad_t[...], jnp.zeros_like(grad_t)], axis=1).astype(F32)
    nodes = (((0,), (0,)), ((), ()))
    partial[0] = lax.dot_general(dst[...], grad, nodes, preferred_element_type=F32)
    partial[1] = lax.dot_general(agg, grad, nodes, preferred_element_type=F32)


def pair_kernel(mine, theirs, pair):
    pair[0] = jnp.where(on_first_core(), mine[...], theirs[...])
    pair[1] = jnp.where(on_first_core(), theirs[...], mine[...])


def weight_fold_kernel(mine, theirs, *rest):
    whole, half = rest[-2:]
    first = (mine[0] + theirs[0]).astype(BF16)
    second = (mine[1] + theirs[1]).astype(BF16)
    whole[0] = first
    whole[1] = second
    half[...] = jnp.where(on_first_core(), first, second)


def weight_rows_kernel(peers, *refs):
    whole, seen, passed = refs[0], refs[1 : 1 + peers], refs[1 + peers : 1 + 2 * peers]
    total, half = refs[-2:]
    terms = peer_terms(on_first_core(), whole, seen, passed)
    sums = [tree_sum([t[h].astype(F32) for t in terms]).astype(BF16) for h in range(2)]
    total[0] = sums[0]
    total[1] = sums[1]
    half[...] = jnp.where(on_first_core(), sums[0], sums[1])


def backward_kernel(peers, groups, *refs):
    rows, cols, counts, values, pair = refs[:5]
    seen, passed = refs[5 : 5 + peers], refs[5 + peers : 5 + 2 * peers]
    own, *sends = refs[5 + 2 * peers : 5 + 2 * peers + groups]
    table, acc = refs[5 + 2 * peers + groups :]
    slots = values.shape[2]
    share = own.shape[0]
    me = lax.axis_index("col") // 2 * 2
    group = lax.axis_index("row")
    for p, term in enumerate(peer_terms(on_first_core(), pair, seen, passed)):
        table[2 * p] = term[0].astype(BF16)
        table[2 * p + 1] = term[1].astype(BF16)
    acc[...] = jnp.zeros_like(acc)
    live = counts[0, 0]
    for s in range(slots):
        block = values[0, 0, s]
        block = jnp.where(s < live, block, jnp.zeros_like(block))
        at = cols[0, 0, s] ^ (group * share)
        acc[at] += jnp.dot(table[rows[0, 0, s] ^ me], block, preferred_element_type=F32)
    own[...] = acc[:share]
    for g in range(1, groups):
        sends[g - 1][...] = acc[g * share : (g + 1) * share].astype(BF16)


def final_kernel(scale, peers, groups, *refs):
    whole, seen, passed = refs[0], refs[1 : 1 + peers], refs[1 + peers : 1 + 2 * peers]
    held = refs[1 + 2 * peers]
    terms = refs[2 + 2 * peers : 2 + 2 * peers + groups]
    output, w_self, w_neigh, out = refs[2 + 2 * peers + groups :]
    output[...] = held[...]
    weights = peer_terms(on_first_core(), whole, seen, passed)
    w_self[...] = tree_sum([t[0].astype(F32) for t in weights]) * scale
    w_neigh[...] = tree_sum([t[1].astype(F32) for t in weights]) * scale
    blocks, _, block = terms[0].shape
    for b in range(blocks):
        total = tree_sum([r[b].astype(F32) for r in terms])
        out[b * block : (b + 1) * block, :] = total.T


def busy(mib):
    return pl.CostEstimate(flops=0, bytes_accessed=mib * 1024 * 1024, transcendentals=0)


def shaped(shape, dtype):
    return jax.ShapeDtypeStruct(shape, dtype)


def per_device(
    features,
    dst_features,
    w_self,
    w_neigh,
    cotangent,
    block_values,
    block_rows,
    block_cols,
    block_counts,
):
    block = block_values.shape[-1]
    width = features.shape[-1]
    hidden = w_self.shape[-1]
    local = dst_features.shape[0]
    col_total = lax.axis_size("col")
    groups = lax.axis_size("row")
    pairs = col_total // 2
    table = features.reshape(-1, block, width)
    source_blocks = table.shape[0]
    params = pltpu.CompilerParams(vmem_limit_bytes=24 * 1024 * 1024)

    inputs = (block_rows, block_cols, block_values, table)
    mine, theirs, rows, cols, values = pl.pallas_call(
        forward_kernel,
        out_shape=[shaped((pairs, block, width), F32)] * 2
        + [shaped(x.shape, x.dtype) for x in (block_rows, block_cols, block_values)],
        in_specs=[HBM, HBM, SMEM, HBM, HBM],
        out_specs=[VMEM] * 5,
        scratch_shapes=[
            pltpu.SMEM(block_rows.shape, jnp.int32),
            pltpu.SMEM(block_cols.shape, jnp.int32),
            pltpu.VMEM(table.shape, BF16),
            pltpu.VMEM((col_total, block, width), F32),
            pltpu.SemaphoreType.DMA((9,)),
        ],
        compiler_params=params,
        name="forward_blocks",
    )(
        *[pltpu.with_memory_space_constraint(x, pltpu.HBM) for x in inputs[:2]],
        block_counts,
        *[pltpu.with_memory_space_constraint(x, pltpu.HBM) for x in inputs[2:]],
    )
    chip_sum = mine + xor_permute(theirs, "col", 1)
    sums = [chip_sum[0]] + [xor_permute(chip_sum[p].astype(BF16), "col", 2 * p) for p in range(1, pairs)]

    held, grad_t, grad_wide, partial = pl.pallas_call(
        functools.partial(middle_kernel, pairs),
        out_shape=[
            shaped((local, hidden), BF16),
            shaped((width, local), BF16),
            shaped((width, 2 * local), F32),
            shaped((2, width, hidden), F32),
        ],
        in_specs=[VMEM] * (pairs + 4),
        out_specs=[VMEM] * 4,
        compiler_params=params,
        name="dense_layer",
    )(*sums, dst_features, w_self, w_neigh, cotangent)
    col_peers, row_peers = pairs // 2, groups // 2
    pair = pl.pallas_call(
        pair_kernel,
        out_shape=shaped((2, width, local), BF16),
        in_specs=[VMEM] * 2,
        out_specs=VMEM,
        compiler_params=params,
        name="gradient_pair",
    )(grad_t, xor_permute(grad_t, "col", 1))
    seen, passed = gather_peers(pair, grad_wide, "col", pairs)

    after = [pair]
    weight, weight_half = pl.pallas_call(
        weight_fold_kernel,
        out_shape=[shaped((2, width, hidden), BF16), shaped((width, hidden), BF16)],
        in_specs=[VMEM] * 2 + [ANY] * len(after),
        out_specs=[VMEM] * 2,
        compiler_params=params,
        name="weight_fold",
    )(partial, xor_permute(partial, "col", 1), *after)
    weight_seen, weight_passed = gather_peers(weight, weight_half, "row", groups)

    source_share = source_blocks // groups
    own, *sends = pl.pallas_call(
        functools.partial(backward_kernel, col_peers, groups),
        out_shape=[shaped((source_share, width, block), F32)]
        + [shaped((source_share, width, block), BF16)] * (groups - 1),
        in_specs=[SMEM, SMEM, SMEM] + [VMEM] * (2 + 2 * col_peers),
        out_specs=[VMEM] * groups,
        scratch_shapes=[
            pltpu.VMEM((col_total, width, block), BF16),
            pltpu.VMEM((source_blocks, width, block), F32),
        ],
        compiler_params=params,
        cost_estimate=busy(32),
        name="backward_blocks",
    )(rows, cols, block_counts, values, pair, *seen, *passed)
    after = [own]
    weight, weight_half = pl.pallas_call(
        functools.partial(weight_rows_kernel, row_peers),
        out_shape=[shaped((2, width, hidden), BF16), shaped((width, hidden), BF16)],
        in_specs=[VMEM] * (1 + 2 * row_peers) + [ANY] * len(after),
        out_specs=[VMEM] * 2,
        compiler_params=params,
        name="weight_rows",
    )(weight, *weight_seen, *weight_passed, *after)
    weight_seen, weight_passed = gather_peers(weight, weight_half, "col", pairs)
    scale = 1.0 / math.sqrt(local * groups * col_total)
    source_terms = [own] + [xor_permute(x, "row", g) for g, x in enumerate(sends, 1)]

    output, grad_self, grad_neigh, grad_source = pl.pallas_call(
        functools.partial(final_kernel, scale, col_peers, groups),
        out_shape=[
            shaped((local, hidden), BF16),
            shaped((width, hidden), F32),
            shaped((width, hidden), F32),
            shaped((source_share * block, width), F32),
        ],
        in_specs=[VMEM] * (2 + 2 * col_peers + groups),
        out_specs=[VMEM] * 4,
        compiler_params=params,
        name="join_outputs",
    )(weight, *weight_seen, *weight_passed, held, *source_terms)
    return output, grad_self, grad_neigh, grad_source.reshape(1, -1, width)


def solution(mesh):
    placed = (
        P("col", None, None),
        P(("row", "col"), None),
        P(),
        P(),
        P(("row", "col"), None),
        P("row", "col", None, None, None),
        P("row", "col", None),
        P("row", "col", None),
        P("row", "col"),
    )
    return jax.shard_map(
        per_device,
        mesh=mesh,
        in_specs=placed,
        out_specs=(P(("row", "col"), None), P(), P(), P("col", "row", None)),
        check_vma=False,
    )
```
